32 devices in a mesh: groups: 2 (over x), pool: 8 (over z, y), tp: 2 (over core).
Axes of the slice: x: 2, y: 2, z: 4, core: 2. Of those that a mesh axis runs over, the one named last changes fastest.
Arguments:
- tokens: bfloat16 [512, 8192], P('groups', 'pool'), parts along dimension 0, may hold values from -300 to 300
- gain: float32 [8192], P('pool'), may hold values from 0.1 to 1.9
- w_query: bfloat16 [8192, 8192], P('pool', 'tp'), may hold values from -0.0625 to 0.0625
- w_key: bfloat16 [8192, 1024], P('pool', 'tp'), may hold values from -0.0625 to 0.0625
- w_value: bfloat16 [8192, 1024], P('pool', 'tp'), may hold values from -0.25 to 0.25
- bias_query: float32 [8192], P('tp'), may hold values from -3 to 3
- bias_key: float32 [1024], P('tp'), may hold values from -3 to 3
- bias_value: float32 [1024], P('tp'), may hold values from -12 to 12
- w_output: bfloat16 [8192, 8192], P('tp', 'pool'), may hold values from -0.0625 to 0.0625
- cache_keys: bfloat16 [512, 160, 1024], P(('groups', 'pool'), None, 'tp'), parts along dimension 0, may hold values from -210 to 210
- cache_values: bfloat16 [512, 160, 1024], P(('groups', 'pool'), None, 'tp'), parts along dimension 0, may hold values from -24 to 24
- lengths: int32 [512], P(('groups', 'pool')), parts along dimension 0, may hold values from 1 to 160, 20480 in all
- request_of_slot: int32 [512], P('groups'), parts along dimension 0, may hold values from 0 to 255, each once
Outputs:
- attn_out: bfloat16 [512, 8192], P(('groups', 'tp'), 'pool'), parts along dimension 0
The draws below stay inside these ranges and needn't reach their ends.
There are 2 independent parts, one for each index of `groups`. The reference program is written for one: setup_inputs(seed, part) draws one part's arguments, and reference() takes and returns one part's arrays. A program takes and returns all parts, laid end to end along the dimension named above; an argument that names none is the same for every part. Nothing has to cross between parts.
Inputs may be any that keep to these rules, and one draw needn't show every extreme that they name: `lengths`: the largest length is exactly 160. `request_of_slot`: a permutation of the 256 requests; slot s is held by cache owner s // 32.
All inputs are finite; a program needn't handle non-finite values. No bound on the sum of `lengths` on one device may be relied on, other than what follows from the above.
Results may differ from the reference program's by a relative error of at most 0.0075.
The reference program's roundings to bfloat16 on the way count: a program that leaves them out, or rounds other values in their place, can miss the bound.
Values may be sent and summed in bfloat16 or wider, within the bound.
A program may use at most 128 MiB of HBM per device.

```python
import math
import jax
import jax.numpy as jnp
import numpy as np
from jax import lax

D = 8192
HEADS = 64
KV_HEADS = 8
HD = 128
CACHE = 160
REQUESTS = 256


def draw_tokens(key, part):
    key = jax.random.fold_in(key, 11)
    first_key, second_key = jax.random.split(key)
    column = jnp.arange(D, dtype=jnp.float32) / D
    base = jnp.clip(jax.random.normal(first_key, (REQUESTS, D), jnp.float32), -5.0, 5.0)
    rowscale = jnp.exp(jax.random.uniform(second_key, (REQUESTS, 1), jnp.float32, 0.0, math.log(10.0)))
    colscale = jnp.exp(column * math.log(3.0))
    return (base * rowscale * colscale[None, :]).astype(jnp.bfloat16)


def draw_cache_keys(key, part):
    key = jax.random.fold_in(key, 23)
    first_key = jax.random.fold_in(key, 0)
    shape = (REQUESTS, CACHE, KV_HEADS * HD)
    base = jnp.clip(jax.random.normal(first_key, shape, jnp.float32), -5.0, 5.0)
    return base.astype(jnp.bfloat16)


def shard_levels(own_key, extent, pieces, least, high):
    loudness, own = 1.0, jax.random.fold_in(own_key, 6)
    for axis_at, blocks in pieces:
        draws = jnp.exp(jax.random.uniform(jax.random.fold_in(own, axis_at), (blocks,), jnp.float32, least / len(pieces), high / len(pieces)))
        loudness = loudness * jnp.repeat(draws, extent[axis_at] // blocks).reshape([-1 if axis == axis_at else 1 for axis in range(len(extent))])
    return loudness


def profile(amount, total, limit, skew):
    weights = [(1 << 20) // math.isqrt(grade ** skew) + 1 for grade in range(2, amount + 1)]
    spare, given = total - limit - (amount - 1), [1] * (amount - 1)
    while spare > 0:
        candidates = [i for i in range(amount - 1) if given[i] < limit]
        pool, remaining = sum([weights[i] for i in candidates]), spare
        for i in candidates:
            extra = min(limit - given[i], max(1, remaining * weights[i] // pool), spare)
            given[i] = given[i] + extra
            spare = spare - extra
    return np.array([limit] + given)


def ragged_sizes(stream_key, amount, total, limit, lean):
    if amount == 2:
        one = jax.random.randint(stream_key, (), max(1, total - limit), min(limit, total - 1) + 1)
        return jnp.stack([one, total - one])
    tallies = jnp.asarray(profile(amount, total, limit, lean), jnp.int32)
    pairs = (amount - 1) // 2
    donor, taker = tallies[1:1 + 2 * pairs:2], tallies[2:2 + 2 * pairs:2]
    margin = jnp.minimum(donor - 1, limit - taker)
    passed = jax.random.randint(jax.random.fold_in(stream_key, 1), (pairs,), 0, 1 << 20) % (margin + 1)
    tallies = tallies.at[1:1 + 2 * pairs:2].set(donor - passed).at[2:2 + 2 * pairs:2].set(taker + passed)
    return tallies[jax.random.permutation(jax.random.fold_in(stream_key, 2), amount)]


def noise(own_key, shape, spread, limit, cuts=(), held_as=jnp.bfloat16):
    entries = spread * jax.random.normal(own_key, shape, jnp.float32)
    if cuts:
        entries = entries * shard_levels(own_key, shape, cuts, -0.22, 0.18)
    return jnp.clip(entries, -limit, limit).astype(held_as)


def setup_inputs(seed: int = 0, part: int = 0) -> dict:
    arg_keys = jax.random.split(jax.random.key(seed), 14)
    own_keys = jax.random.split(jax.random.fold_in(arg_keys[13], part), 14)
    tokens = draw_tokens(jax.random.fold_in(jax.random.fold_in(arg_keys[13], part), 71), part)
    gain = jnp.clip(1.0 + 0.18 * jax.random.normal(arg_keys[1], (D,), jnp.float32), 0.1, 1.9)
    w_query = noise(arg_keys[2], (D, HEADS * HD), D ** -0.5, 0.0625, ((0, 8), (1, 2)))
    w_key = noise(arg_keys[3], (D, KV_HEADS * HD), D ** -0.5, 0.0625, ((0, 8), (1, 2)))
    w_value = noise(arg_keys[4], (D, KV_HEADS * HD), (D // 16) ** -0.5, 0.25, ((0, 8), (1, 2)))
    bias_query = noise(arg_keys[5], (HEADS * HD,), 0.5, 3.0, ((0, 2),), jnp.float32)
    bias_key = noise(arg_keys[6], (KV_HEADS * HD,), 0.5, 3.0, ((0, 2),), jnp.float32)
    bias_value = noise(arg_keys[7], (KV_HEADS * HD,), 2.0, 12.0, ((0, 2),), jnp.float32)
    w_output = noise(arg_keys[8], (HEADS * HD, D), (HEADS * HD) ** -0.5, 0.0625, ((0, 2), (1, 8)))
    cache_keys = draw_cache_keys(jax.random.fold_in(jax.random.fold_in(arg_keys[13], part), 71), part)
    cache_values = noise(own_keys[10], (REQUESTS, CACHE, KV_HEADS * HD), 4.0, 24.0, ((0, 8), (2, 2)))
    lengths = ragged_sizes(own_keys[11], REQUESTS, REQUESTS * CACHE // 2, CACHE, 2).astype(jnp.int32)
    request_of_slot = jax.random.permutation(own_keys[12], REQUESTS).astype(jnp.int32)
    return {"tokens": tokens, "gain": gain, "w_query": w_query, "w_key": w_key, "w_value": w_value, "bias_query": bias_query, "bias_key": bias_key, "bias_value": bias_value, "w_output": w_output, "cache_keys": cache_keys, "cache_values": cache_values, "lengths": lengths, "request_of_slot": request_of_slot}


ROPE_BASE = 1000000.0
EPSILON = 1e-06
NEGATIVE = -1e+30

def rotate(vectors, positions):
    halfway = vectors.shape[-1] // 2
    index = jnp.arange(halfway, dtype=jnp.float32)
    freqs = ROPE_BASE ** (-2.0 * index / vectors.shape[-1])
    angles = positions.astype(jnp.float32)[:, None] * freqs[None, :]
    cosine = jnp.cos(angles)[:, None, :]
    sine = jnp.sin(angles)[:, None, :]
    former = vectors[..., :halfway]
    latter = vectors[..., halfway:]
    return jnp.concatenate([former * cosine - latter * sine, latter * cosine + former * sine], axis=-1)

def attend_one(inputs):
    query, key_new, value_new, keys, values, length = inputs
    kv_count = key_new.shape[0]
    grouped = query.astype(jnp.float32).reshape(kv_count, -1, HD)
    cached_k = keys.astype(jnp.float32).reshape(CACHE, kv_count, HD)
    cached_v = values.astype(jnp.float32).reshape(CACHE, kv_count, HD)
    scaling = HD ** (-0.5)
    older = jnp.einsum('kgd,ckd->kgc', grouped, cached_k) * scaling
    filled = jnp.arange(CACHE) < length
    older = jnp.where(filled[None, None, :], older, NEGATIVE)
    newest = jnp.einsum('kgd,kd->kg', grouped, key_new.astype(jnp.float32)) * scaling
    highest = jnp.maximum(lax.optimization_barrier(jnp.max(older, axis=-1)), newest)
    w_old = jnp.exp(older - highest[..., None])
    w_new = jnp.exp(newest - highest)
    denominator = lax.optimization_barrier(jnp.sum(w_old, axis=-1)) + w_new
    p_old = (w_old / denominator[..., None]).astype(jnp.bfloat16)
    p_new = (w_new / denominator).astype(jnp.bfloat16)
    context = jnp.einsum('kgc,ckd->kgd', p_old.astype(jnp.float32), cached_v)
    context = context + p_new.astype(jnp.float32)[..., None] * value_new.astype(jnp.float32)[:, None, :]
    return context.reshape(-1).astype(jnp.bfloat16)

def reference(tokens, gain, w_query, w_key, w_value, bias_query, bias_key, bias_value, w_output, cache_keys, cache_values, lengths, request_of_slot):
    ordered = jnp.take(tokens, request_of_slot, axis=0)
    widened = ordered.astype(jnp.float32)
    squares = lax.optimization_barrier(jnp.sum(widened * widened, axis=1))
    inverse = 1.0 / jnp.sqrt(squares / D + EPSILON)
    scaled = (widened * gain[None, :]).astype(jnp.bfloat16)
    query = jnp.dot(scaled, w_query, preferred_element_type=jnp.float32) * inverse[:, None] + bias_query
    key_new = jnp.dot(scaled, w_key, preferred_element_type=jnp.float32) * inverse[:, None] + bias_key
    value_new = jnp.dot(scaled, w_value, preferred_element_type=jnp.float32) * inverse[:, None] + bias_value
    rotated_query = rotate(query.reshape(REQUESTS, HEADS, HD), lengths).astype(jnp.bfloat16)
    rotated_key = rotate(key_new.reshape(REQUESTS, KV_HEADS, HD), lengths).astype(jnp.bfloat16)
    new_value = value_new.reshape(REQUESTS, KV_HEADS, HD).astype(jnp.bfloat16)
    context = lax.map(attend_one, (rotated_query, rotated_key, new_value, cache_keys, cache_values, lengths))
    slot_of = jnp.zeros((REQUESTS,), jnp.int32).at[request_of_slot].set(jnp.arange(REQUESTS, dtype=jnp.int32))
    by_request = jnp.take(context, slot_of, axis=0)
    return jnp.dot(by_request, w_output, preferred_element_type=jnp.float32).astype(jnp.bfloat16)
```

```python
import functools
import jax
import jax.numpy as jnp
from jax import lax
from jax.experimental import pallas as pl
from jax.experimental.pallas import tpu as pltpu
from jax.sharding import PartitionSpec as P

D = 8192
HD = 128


ROPE_BASE = 1000000.0
EPSILON = 1e-06
NEGATIVE = -1e30
MIB = 1 << 20
LEVELS = 32000.0


def greet(devices):
    barrier = pltpu.get_barrier_semaphore()
    for device in devices:
        pl.semaphore_signal(
            barrier, inc=1, device_id=device, device_id_type=pl.DeviceIdType.MESH
        )
    pl.semaphore_wait(barrier, len(devices))


def remote(src, dst, send, recv, device):
    return pltpu.make_async_remote_copy(
        src_ref=src,
        dst_ref=dst,
        send_sem=send,
        recv_sem=recv,
        device_id=device,
        device_id_type=pl.DeviceIdType.MESH,
    )


def lane(stats, c):
    index = lax.broadcasted_iota(jnp.int32, stats.shape, 1)
    return jnp.sum(jnp.where(index == c, stats, 0.0), axis=1, keepdims=True)


def with_lane(stats, c, column):
    index = lax.broadcasted_iota(jnp.int32, stats.shape, 1)
    return jnp.where(index == c, column, stats)


def encode(values, bound):
    factor = jnp.where(bound > 1e-30, LEVELS / jnp.maximum(bound, 1e-30), 0.0)
    return jnp.round(values * factor).astype(jnp.int32).astype(jnp.int16)


def decode(codes, bound):
    return codes.astype(jnp.int32).astype(jnp.float32) * (bound * (1.0 / LEVELS))


def layer_kernel(
    pairs,
    lengths,
    slots,
    tokens,
    gain,
    cosine,
    sine,
    bias,
    w_query,
    w_key,
    w_value,
    w_output,
    cache_keys,
    cache_values,
    out,
    weights,
    chosen,
    x,
    squares,
    mine,
    near_out,
    near_in,
    far_in,
    near_stat_out,
    near_stat_in,
    stat_sum,
    far_stat_in,
    keys,
    values,
    heads,
    key_new,
    value_new,
    out_weights,
    gathered,
    acc,
    across,
    w_sem,
    near_send,
    near_recv,
    far_send,
    far_recv,
    stat_sem,
    far_stat_send,
    far_stat_recv,
    cache_sem,
    out_w_sem,
    ctx_far_send,
    ctx_far_recv,
    ctx_near_send,
    ctx_near_recv,
    tp_sem,
):
    me = lax.axis_index("pool")
    half = lax.axis_index("tp")
    place, side = me // 2, me % 2
    chunks, depth, width = weights.shape
    query_chunks = chunks - 2
    _, _, rows, _ = mine.shape
    count = pairs * rows
    total_rows = 2 * count
    per_chunk = width // HD
    head_count = query_chunks * per_chunk
    group = head_count // per_chunk
    span = keys.shape[1]
    batches, batch = cache_sem.shape[1], rows // cache_sem.shape[1]
    partner = {"pool": place * 2 + 1 - side}
    other_core = {"tp": 1 - half}
    peers = [{"pool": lax.rem(place + d, pairs) * 2 + side} for d in range(1, pairs)]

    def query_load(c):
        columns = pl.ds(pl.multiple_of(c * width, width), width)
        return pltpu.make_async_copy(w_query.at[:, columns], weights.at[c], w_sem.at[c])

    def out_load(c):
        part = pl.ds(pl.multiple_of(c * width, width), width)
        return pltpu.make_async_copy(w_output.at[part, :], out_weights.at[c], out_w_sem.at[c])

    def cache_load(b, which):
        source, target = ((cache_keys, keys), (cache_values, values))[which]
        part = pl.ds(b * batch, batch)
        return pltpu.make_async_copy(source.at[part], target.at[part], cache_sem.at[which, b])

    def near(c):
        return remote(
            near_out.at[c], near_in.at[c], near_send.at[c], near_recv.at[c], partner
        )

    def far(c, d):
        return remote(
            near_in.at[c, lax.rem(place + d, pairs)],
            far_in.at[c, d - 1],
            far_send.at[c, d - 1],
            far_recv.at[c, d - 1],
            peers[d - 1],
        )

    def far_stat(d):
        return remote(
            stat_sum.at[lax.rem(place + d, pairs)],
            far_stat_in.at[d - 1],
            far_stat_send.at[d - 1],
            far_stat_recv.at[d - 1],
            peers[d - 1],
        )

    def ctx_far(c, d, source):
        slot = gathered.at[c, source, side]
        return remote(
            slot, slot, ctx_far_send.at[c, d - 1], ctx_far_recv.at[c, d - 1], peers[d - 1]
        )

    def ctx_near(c, which):
        slot = gathered.at[c, :, which]
        return remote(slot, slot, ctx_near_send.at[c], ctx_near_recv.at[c], partner)

    @pl.loop(0, query_chunks)
    def _(c):
        query_load(c).start()

    key_load = pltpu.make_async_copy(w_key, weights.at[chunks - 2], w_sem.at[chunks - 2])
    value_load = pltpu.make_async_copy(w_value, weights.at[chunks - 1], w_sem.at[chunks - 1])
    key_load.start()
    value_load.start()

    @pl.loop(0, batches)
    def _(b):
        cache_load(b, 0).start()
        cache_load(b, 1).start()

    @pl.loop(0, query_chunks)
    def _(c):
        out_load(c).start()

    requests = lax.broadcasted_iota(jnp.int32, (total_rows, total_rows), 0)
    chosen[...] = jnp.where(requests == slots[...], 1.0, 0.0).astype(jnp.bfloat16)
    ordered = lax.dot_general(
        chosen[...], tokens[...], (((0,), (0,)), ((), ())), preferred_element_type=jnp.float32
    )
    square = jnp.sum(ordered * ordered, axis=1, keepdims=True)
    squares[...] = jnp.broadcast_to(square, (total_rows, HD)).reshape(squares.shape)
    x[...] = (ordered * gain[...]).astype(jnp.bfloat16).reshape(x.shape)
    greet([partner, other_core] + peers)

    near_stat_out[...] = squares[:, 1 - side].reshape(count, HD)
    stat_sum[...] = squares[:, side]

    @pl.loop(0, chunks)
    def _(c):
        pltpu.make_async_copy(weights.at[c], weights.at[c], w_sem.at[c]).wait()
        part = jnp.dot(
            x[:, 1 - side].reshape(count, depth), weights[c], preferred_element_type=jnp.float32
        )
        bound = jnp.max(jnp.abs(part), axis=1, keepdims=True)
        near_stat_out[...] = with_lane(near_stat_out[...], c, bound)
        near_out[c] = encode(part, bound).reshape(pairs, rows, width)

    stat_copy = remote(near_stat_out, near_stat_in, stat_sem.at[0], stat_sem.at[1], partner)
    stat_copy.start()

    @pl.loop(0, chunks)
    def _(c):
        near(c).start()

    @pl.loop(0, chunks)
    def _(c):
        part = jnp.dot(
            x[:, side].reshape(count, depth), weights[c], preferred_element_type=jnp.float32
        )
        bound = jnp.max(jnp.abs(part), axis=1, keepdims=True)
        stat_sum[...] = with_lane(
            stat_sum[...].reshape(count, HD), c, bound
        ).reshape(stat_sum.shape)
        mine[c] = part.reshape(pairs, rows, width)

    stat_copy.wait()
    stat_sum[...] = stat_sum[...] + near_stat_in[...].reshape(stat_sum.shape)
    for d in range(1, pairs):
        far_stat(d).start()

    @pl.loop(0, chunks)
    def _(c):
        near(c).wait_recv()
        both = mine[c].reshape(count, width) + decode(
            near_in[c].reshape(count, width), lane(near_stat_in[...], c)
        )
        mine[c] = both.reshape(pairs, rows, width)
        bound = lane(stat_sum[...].reshape(count, HD), c)
        near_in[c] = encode(both, bound).reshape(pairs, rows, width)
        for d in range(1, pairs):
            far(c, d).start()

    square_sum = lane(stat_sum[place], HD - 1)
    for d in range(1, pairs):
        far_stat(d).wait_recv()
        square_sum = square_sum + lane(far_stat_in[d - 1], HD - 1)
    inverse = 1.0 / jnp.sqrt(square_sum / (depth * pairs * 2) + EPSILON)

    def finish(c):
        total = mine[c, place]
        for d in range(1, pairs):
            far(c, d).wait_recv()
            total = total + decode(far_in[c, d - 1], lane(far_stat_in[d - 1], c))
        return total * inverse + bias[pl.ds(c, 1), :]

    def turned(vectors, j):
        one = vectors[:, j * HD : (j + 1) * HD]
        return one * cosine[...] + pltpu.roll(one, HD // 2, 1) * sine[...]

    @pl.loop(0, query_chunks)
    def _(c):
        query = finish(c)
        for j in range(per_chunk):
            heads[pl.ds(c * per_chunk + j, rows, stride=head_count), :] = turned(query, j)

    key = finish(chunks - 2)
    key_new[...] = jnp.concatenate(
        [turned(key, j) for j in range(per_chunk)], axis=1
    ).astype(jnp.bfloat16).astype(jnp.float32)
    value_new[...] = finish(chunks - 1).astype(jnp.bfloat16).astype(jnp.float32)

    of_row = lax.broadcasted_iota(jnp.int32, (head_count, width), 0) // group
    of_column = lax.broadcasted_iota(jnp.int32, (head_count, width), 1) // HD
    same = of_row == of_column
    position = lax.broadcasted_iota(jnp.int32, (head_count, span), 1)
    scaling = HD ** (-0.5)

    def attend(n):
        own = pl.ds(pl.multiple_of(n * head_count, head_count), head_count)
        query = heads[own, :].astype(jnp.bfloat16).astype(jnp.float32)
        spread = jnp.where(same, jnp.concatenate([query] * per_chunk, axis=1), 0.0)
        older = lax.dot_general(
            spread.astype(jnp.bfloat16),
            keys[n],
            (((1,), (1,)), ((), ())),
            preferred_element_type=jnp.float32,
        ) * scaling
        newest = jnp.sum(spread * key_new[pl.ds(n, 1), :], axis=1, keepdims=True) * scaling
        older = jnp.where(position < lengths[n], older, NEGATIVE)
        highest = jnp.maximum(jnp.max(older, axis=1, keepdims=True), newest)
        w_old = jnp.exp(older - highest)
        w_new = jnp.exp(newest - highest)
        denominator = jnp.sum(w_old, axis=1, keepdims=True) + w_new
        p_old = (w_old / denominator).astype(jnp.bfloat16)
        p_new = (w_new / denominator).astype(jnp.bfloat16).astype(jnp.float32)
        context = jnp.dot(p_old, values[n], preferred_element_type=jnp.float32)
        context = context + p_new * value_new[pl.ds(n, 1), :]
        heads[own, :] = jnp.concatenate(
            [
                context[k * group : (k + 1) * group, k * HD : (k + 1) * HD]
                for k in range(per_chunk)
            ],
            axis=0,
        )

    @pl.loop(0, batches)
    def _(b):
        cache_load(b, 0).wait()
        cache_load(b, 1).wait()
        for j in range(batch):
            attend(b * batch + j)

    @pl.loop(0, query_chunks)
    def _(c):
        gathered[c, place, side] = jnp.concatenate(
            [
                heads[pl.ds(c * per_chunk + j, rows, stride=head_count), :]
                for j in range(per_chunk)
            ],
            axis=1,
        ).astype(jnp.bfloat16)
        for d in range(1, pairs):
            ctx_far(c, d, place).start()

    acc[...] = jnp.zeros_like(acc)

    def multiply(c):
        ctx_near(c, 1 - side).wait_recv()
        out_load(c).wait()
        by_request = jnp.dot(
            chosen[...],
            gathered[c].reshape(total_rows, width),
            preferred_element_type=jnp.float32,
        ).astype(jnp.bfloat16)
        acc[...] += jnp.dot(
            by_request, out_weights[c], preferred_element_type=jnp.float32
        ).reshape(acc.shape)

    @pl.loop(0, query_chunks)
    def _(c):
        for d in range(1, pairs):
            ctx_far(c, d, lax.rem(place + pairs - d, pairs)).wait_recv()
        ctx_near(c, side).start()

        @pl.when(c > 0)
        def _():
            multiply(c - 1)

    multiply(query_chunks - 1)
    swap = remote(acc.at[1 - half], across, tp_sem.at[0], tp_sem.at[1], other_core)
    swap.start()

    @pl.loop(0, chunks)
    def _(c):
        near(c).wait_send()
        for d in range(1, pairs):
            far(c, d).wait_send()

    @pl.loop(0, query_chunks)
    def _(c):
        ctx_near(c, side).wait_send()
        for d in range(1, pairs):
            ctx_far(c, d, place).wait_send()

    for d in range(1, pairs):
        far_stat(d).wait_send()
    swap.wait()
    out[...] = (acc[half] + across[...]).astype(jnp.bfloat16)


def local(
    tokens,
    gain,
    w_query,
    w_key,
    w_value,
    bias_query,
    bias_key,
    bias_value,
    w_output,
    cache_keys,
    cache_values,
    lengths,
    request_of_slot,
):
    pairs = lax.axis_size("pool") // 2
    total_rows, depth = tokens.shape
    count = total_rows // 2
    rows = count // pairs
    width = w_key.shape[1]
    query_chunks = w_query.shape[1] // width
    chunks = query_chunks + 2
    head_count = w_query.shape[1] // HD
    span = cache_keys.shape[1]
    columns = w_output.shape[1]
    batches = rows // 4
    index = jnp.arange(HD // 2, dtype=jnp.float32)
    freqs = ROPE_BASE ** (-2.0 * index / HD)
    angles = lengths.astype(jnp.float32)[:, None] * freqs[None, :]
    cosine, sine = jnp.cos(angles), jnp.sin(angles)
    cosine = jnp.concatenate([cosine, cosine], axis=1)
    sine = jnp.concatenate([-sine, sine], axis=1)
    bias = jnp.concatenate([bias_query, bias_key, bias_value]).reshape(chunks, width)
    vmem = pl.BlockSpec(memory_space=pltpu.VMEM)
    hbm = pl.BlockSpec(memory_space=pl.ANY)
    dma = pltpu.SemaphoreType.DMA
    bf16, f32, i16 = jnp.bfloat16, jnp.float32, jnp.int16
    return pl.pallas_call(
        functools.partial(layer_kernel, pairs),
        out_shape=jax.ShapeDtypeStruct((count, columns), bf16),
        in_specs=[pl.BlockSpec(memory_space=pltpu.SMEM)] + [vmem] * 6 + [hbm] * 6,
        out_specs=vmem,
        scratch_shapes=[
            pltpu.VMEM((chunks, depth, width), bf16),
            pltpu.VMEM((total_rows, total_rows), bf16),
            pltpu.VMEM((pairs, 2, rows, depth), bf16),
            pltpu.VMEM((pairs, 2, rows, HD), f32),
            pltpu.VMEM((chunks, pairs, rows, width), f32),
            pltpu.VMEM((chunks, pairs, rows, width), i16),
            pltpu.VMEM((chunks, pairs, rows, width), i16),
            pltpu.VMEM((chunks, pairs - 1, rows, width), i16),
            pltpu.VMEM((count, HD), f32),
            pltpu.VMEM((count, HD), f32),
            pltpu.VMEM((pairs, rows, HD), f32),
            pltpu.VMEM((pairs - 1, rows, HD), f32),
            pltpu.VMEM((rows, span, width), bf16),
            pltpu.VMEM((rows, span, width), bf16),
            pltpu.VMEM((rows * head_count, HD), f32),
            pltpu.VMEM((rows, width), f32),
            pltpu.VMEM((rows, width), f32),
            pltpu.VMEM((query_chunks, width, columns), bf16),
            pltpu.VMEM((query_chunks, pairs, 2, rows, width), bf16),
            pltpu.VMEM((2, count, columns), f32),
            pltpu.VMEM((count, columns), f32),
            dma((chunks,)),
            dma((chunks,)),
            dma((chunks,)),
            dma((chunks, pairs - 1)),
            dma((chunks, pairs - 1)),
            dma((2,)),
            dma((pairs - 1,)),
            dma((pairs - 1,)),
            dma((2, batches)),
            dma((query_chunks,)),
            dma((query_chunks, pairs - 1)),
            dma((query_chunks, pairs - 1)),
            dma((query_chunks,)),
            dma((query_chunks,)),
            dma((2,)),
        ],
        compiler_params=pltpu.CompilerParams(
            collective_id=0, has_side_effects=True, vmem_limit_bytes=62 * MIB
        ),
        cost_estimate=pl.CostEstimate(
            flops=4 * total_rows * depth * chunks * width,
            bytes_accessed=2 * depth * chunks * width + 4 * rows * span * width,
            transcendentals=rows * head_count * span,
        ),
    )(
        lengths,
        request_of_slot[None, :],
        tokens,
        gain[None, :],
        cosine,
        sine,
        bias,
        w_query,
        w_key,
        w_value,
        w_output,
        cache_keys,
        cache_values,
    )


def solution(mesh):
    in_specs = (
        P("groups", "pool"),
        P("pool"),
        P("pool", "tp"),
        P("pool", "tp"),
        P("pool", "tp"),
        P("tp"),
        P("tp"),
        P("tp"),
        P("tp", "pool"),
        P(("groups", "pool"), None, "tp"),
        P(("groups", "pool"), None, "tp"),
        P(("groups", "pool")),
        P("groups"),
    )
    out_specs = P(("groups", "tp"), "pool")
    return jax.shard_map(local, mesh=mesh, in_specs=in_specs, out_specs=out_specs, check_vma=False)
```

```python
import functools
import math
import jax
import jax.numpy as jnp
from jax import lax
from jax.experimental import pallas as pl
from jax.experimental.pallas import tpu as pltpu
from jax.sharding import PartitionSpec as P

D = 8192
HD = 128


ROPE_BASE = 1000000.0
EPSILON = 1e-06
NEGATIVE = -1e30
MIB = 1 << 20
LEVELS = 32000.0


def greet(devices):
    barrier = pltpu.get_barrier_semaphore()
    for device in devices:
        pl.semaphore_signal(
            barrier, inc=1, device_id=device, device_id_type=pl.DeviceIdType.MESH
        )
    pl.semaphore_wait(barrier, len(devices))


def remote(src, dst, send, recv, device):
    return pltpu.make_async_remote_copy(
        src_ref=src,
        dst_ref=dst,
        send_sem=send,
        recv_sem=recv,
        device_id=device,
        device_id_type=pl.DeviceIdType.MESH,
    )


def lane(stats, c):
    index = lax.broadcasted_iota(jnp.int32, stats.shape, 1)
    return jnp.sum(jnp.where(index == c, stats, 0.0), axis=1, keepdims=True)


def with_lane(stats, c, column):
    index = lax.broadcasted_iota(jnp.int32, stats.shape, 1)
    return jnp.where(index == c, column, stats)


def encode(values, bound):
    factor = jnp.where(bound > 1e-30, LEVELS / jnp.maximum(bound, 1e-30), 0.0)
    return jnp.round(values * factor).astype(jnp.int32).astype(jnp.int16)


def decode(codes, bound):
    return codes.astype(jnp.int32).astype(jnp.float32) * (bound * (1.0 / LEVELS))


def layer_kernel(
    pairs,
    lengths,
    lengths_row,
    slots,
    tokens,
    gain,
    bias_query,
    bias_key,
    bias_value,
    w_query,
    w_key,
    w_value,
    w_output,
    cache_keys,
    cache_values,
    out,
    weights,
    chosen,
    x,
    squares,
    mine,
    near_out,
    near_in,
    far_in,
    near_stat_out,
    near_stat_in,
    stat_sum,
    far_stat_in,
    keys,
    values,
    heads,
    turns,
    key_new,
    value_new,
    out_weights,
    gathered,
    acc,
    across,
    w_sem,
    near_send,
    near_recv,
    far_send,
    far_recv,
    stat_sem,
    far_stat_send,
    far_stat_recv,
    cache_sem,
    out_w_sem,
    ctx_far_send,
    ctx_far_recv,
    ctx_near_send,
    ctx_near_recv,
    tp_sem,
):
    me = lax.axis_index("pool")
    half = lax.axis_index("tp")
    place, side = me // 2, me % 2
    chunks, depth, width = weights.shape
    query_chunks = chunks - 2
    _, _, rows, _ = mine.shape
    count = pairs * rows
    total_rows = 2 * count
    per_chunk = width // HD
    stages, per_stage, _ = heads.shape
    group = per_stage // rows
    step = query_chunks // stages
    first = 2 + step
    span = keys.shape[1]
    batch = 8
    partner = {"pool": place * 2 + 1 - side}
    other_core = {"tp": 1 - half}
    peers = [{"pool": lax.rem(place + d, pairs) * 2 + side} for d in range(1, pairs)]

    def query_load(c):
        columns = pl.ds(pl.multiple_of((c - 2) * width, width), width)
        return pltpu.make_async_copy(w_query.at[:, columns], weights.at[c], w_sem.at[c])

    def out_load(c):
        part = pl.ds(pl.multiple_of(c * width, width), width)
        return pltpu.make_async_copy(w_output.at[part, :], out_weights.at[c], out_w_sem.at[c])

    def near(c):
        return remote(
            near_out.at[c], near_in.at[c], near_send.at[c], near_recv.at[c], partner
        )

    def near_stat(g):
        return remote(
            near_stat_out.at[g], near_stat_in.at[g], stat_sem.at[0, g], stat_sem.at[1, g], partner
        )

    def far(c, d):
        return remote(
            near_in.at[c, lax.rem(place + d, pairs)],
            far_in.at[c, d - 1],
            far_send.at[c, d - 1],
            far_recv.at[c, d - 1],
            peers[d - 1],
        )

    def far_stat(g, d):
        return remote(
            stat_sum.at[g, lax.rem(place + d, pairs)],
            far_stat_in.at[g, d - 1],
            far_stat_send.at[g, d - 1],
            far_stat_recv.at[g, d - 1],
            peers[d - 1],
        )

    def ctx_far(c, d, source):
        slot = gathered.at[c, source, side]
        return remote(
            slot, slot, ctx_far_send.at[c, d - 1], ctx_far_recv.at[c, d - 1], peers[d - 1]
        )

    def ctx_near(c, which):
        slot = gathered.at[c, :, which]
        return remote(slot, slot, ctx_near_send.at[c], ctx_near_recv.at[c], partner)

    key_load = pltpu.make_async_copy(w_key, weights.at[0], w_sem.at[0])
    value_load = pltpu.make_async_copy(w_value, weights.at[1], w_sem.at[1])
    key_load.start()
    value_load.start()

    @pl.loop(2, chunks)
    def _(c):
        query_load(c).start()

    requests = lax.broadcasted_iota(jnp.int32, (total_rows, total_rows), 0)
    chosen[...] = jnp.where(requests == slots[...], 1.0, 0.0).astype(jnp.bfloat16)
    ordered = lax.dot_general(
        chosen[...], tokens[...], (((0,), (0,)), ((), ())), preferred_element_type=jnp.float32
    )
    square = jnp.sum(ordered * ordered, axis=1, keepdims=True)
    squares[...] = jnp.broadcast_to(square, (total_rows, HD)).reshape(squares.shape)
    x[...] = (ordered * gain[...]).astype(jnp.bfloat16).reshape(x.shape)
    greet([partner, other_core] + peers)

    for g, start, stop in ((0, 0, first), (1, first, chunks)):
        near_stat_out[g] = squares[:, 1 - side].reshape(count, HD)

        @pl.loop(start, stop)
        def _(c):
            pltpu.make_async_copy(weights.at[c], weights.at[c], w_sem.at[c]).wait()
            part = jnp.dot(
                x[:, 1 - side].reshape(count, depth),
                weights[c],
                preferred_element_type=jnp.float32,
            )
            bound = jnp.max(jnp.abs(part), axis=1, keepdims=True)
            near_stat_out[g] = with_lane(near_stat_out[g], c, bound)
            near_out[c] = encode(part, bound).reshape(pairs, rows, width)

        near_stat(g).start()

        @pl.loop(start, stop)
        def _(c):
            near(c).start()

    key_cache_load = pltpu.make_async_copy(cache_keys, keys, cache_sem.at[0])
    value_cache_load = pltpu.make_async_copy(cache_values, values, cache_sem.at[1])
    key_cache_load.start()
    value_cache_load.start()

    @pl.loop(0, query_chunks)
    def _(c):
        out_load(c).start()

    for g, start, stop in ((0, 0, first), (1, first, chunks)):
        stat_sum[g] = squares[:, side]

        @pl.loop(start, stop)
        def _(c):
            part = jnp.dot(
                x[:, side].reshape(count, depth), weights[c], preferred_element_type=jnp.float32
            )
            bound = jnp.max(jnp.abs(part), axis=1, keepdims=True)
            stat_sum[g] = with_lane(stat_sum[g].reshape(count, HD), c, bound).reshape(
                pairs, rows, HD
            )
            mine[c] = part.reshape(pairs, rows, width)

    def bounds(g):
        near_stat(g).wait_recv()
        stat_sum[g] = stat_sum[g] + near_stat_in[g].reshape(pairs, rows, HD)
        for d in range(1, pairs):
            far_stat(g, d).start()

    def middle(g, c):
        near(c).wait_recv()
        both = mine[c].reshape(count, width) + decode(
            near_in[c].reshape(count, width), lane(near_stat_in[g], c)
        )
        mine[c] = both.reshape(pairs, rows, width)
        bound = lane(stat_sum[g].reshape(count, HD), c)
        near_in[c] = encode(both, bound).reshape(pairs, rows, width)
        for d in range(1, pairs):
            far(c, d).start()

    bounds(0)

    @pl.loop(0, first)
    def _(c):
        middle(0, c)

    bounds(1)

    here = lax.broadcasted_iota(jnp.int32, (rows, rows), 0)
    there = lax.broadcasted_iota(jnp.int32, (rows, rows), 1)
    length = jnp.sum(
        jnp.where(here == there, lengths_row[...].astype(jnp.float32), 0.0), axis=1, keepdims=True
    )
    index = lax.broadcasted_iota(jnp.int32, (rows, HD), 1)
    index = jnp.where(index < HD // 2, index, index - HD // 2).astype(jnp.float32)
    angles = length * jnp.exp(index * (-2.0 * math.log(ROPE_BASE) / HD))
    sign = jnp.where(lax.broadcasted_iota(jnp.int32, (rows, HD), 1) < HD // 2, -1.0, 1.0)
    turns[0] = jnp.cos(angles)
    turns[1] = jnp.sin(angles) * sign

    square_sum = lane(stat_sum[0, place], HD - 1)
    for d in range(1, pairs):
        far_stat(0, d).wait_recv()
        square_sum = square_sum + lane(far_stat_in[0, d - 1], HD - 1)
    turns[2] = jnp.broadcast_to(
        1.0 / jnp.sqrt(square_sum / (depth * pairs * 2) + EPSILON), (rows, HD)
    )

    def finish(g, c, bias):
        total = mine[c, place]
        for d in range(1, pairs):
            far(c, d).wait_recv()
            total = total + decode(far_in[c, d - 1], lane(far_stat_in[g, d - 1], c))
        return total * turns[2, :, 0:1] + bias

    def turned(vectors, j):
        one = vectors[:, j * HD : (j + 1) * HD]
        return one * turns[0] + pltpu.roll(one, HD // 2, 1) * turns[1]

    key = finish(0, 0, bias_key[...])
    for j in range(stages):
        key_new[j] = turned(key, j).astype(jnp.bfloat16).astype(jnp.float32)
    value = finish(0, 1, bias_value[...])
    for j in range(stages):
        value_new[j] = value[:, j * HD : (j + 1) * HD].astype(jnp.bfloat16).astype(jnp.float32)

    position = lax.broadcasted_iota(jnp.int32, (group, span), 1)
    scaling = HD ** (-0.5)

    def repeated(ref, k, n):
        return jnp.concatenate(
            [jnp.broadcast_to(ref[k, pl.ds(n + j, 1), :], (group, HD)) for j in range(batch)],
            axis=0,
        )

    def attend(k, b):
        n = b * batch
        columns = pl.ds(pl.multiple_of(k * HD, HD), HD)
        own = pl.ds(pl.multiple_of(n * group, batch * group), batch * group)
        query = heads[k, own, :].astype(jnp.bfloat16).astype(jnp.float32)
        scores = []
        for j in range(batch):
            score = lax.dot_general(
                query[j * group : (j + 1) * group].astype(jnp.bfloat16),
                keys[n + j, :, columns],
                (((1,), (1,)), ((), ())),
                preferred_element_type=jnp.float32,
            )
            scores.append(jnp.where(position < lengths[n + j], score * scaling, NEGATIVE))
        older = jnp.concatenate(scores, axis=0)
        newest = jnp.sum(query * repeated(key_new, k, n), axis=1, keepdims=True) * scaling
        highest = jnp.maximum(jnp.max(older, axis=1, keepdims=True), newest)
        w_old = jnp.exp(older - highest)
        w_new = jnp.exp(newest - highest)
        denominator = jnp.sum(w_old, axis=1, keepdims=True) + w_new
        p_old = w_old / denominator
        p_new = (w_new / denominator).astype(jnp.bfloat16).astype(jnp.float32)
        context = jnp.concatenate(
            [
                jnp.dot(
                    p_old[j * group : (j + 1) * group].astype(jnp.bfloat16),
                    values[n + j, :, columns],
                    preferred_element_type=jnp.float32,
                )
                for j in range(batch)
            ],
            axis=0,
        )
        heads[k, own, :] = context + p_new * repeated(value_new, k, n)

    def forward(c):
        for d in range(1, pairs):
            ctx_far(c, d, lax.rem(place + pairs - d, pairs)).wait_recv()
        ctx_near(c, side).start()

    acc[...] = jnp.zeros_like(acc)

    def multiply(c):
        ctx_near(c, 1 - side).wait_recv()
        out_load(c).wait()
        by_request = jnp.dot(
            chosen[...],
            gathered[c].reshape(total_rows, width),
            preferred_element_type=jnp.float32,
        ).astype(jnp.bfloat16)
        acc[...] += jnp.dot(
            by_request, out_weights[c], preferred_element_type=jnp.float32
        ).reshape(acc.shape)

    key_cache_load.wait()
    value_cache_load.wait()

    @pl.loop(0, stages)
    def _(k):
        @pl.when(k < stages - 1)
        def _():
            @pl.loop(0, step)
            def _(i):
                middle(1, first + k * step + i)

        @pl.when(k == 1)
        def _():
            for d in range(1, pairs):
                far_stat(1, d).wait_recv()

        g = (k + stages - 2) // (stages - 1)

        @pl.loop(0, step)
        def _(i):
            c = k * step + i
            columns = pl.ds(pl.multiple_of(c * width, width), width)
            query = finish(g, 2 + c, bias_query[:, columns])
            for j in range(per_chunk):
                heads[k, pl.ds(i * per_chunk + j, rows, stride=group), :] = turned(query, j)

        @pl.loop(0, rows // batch)
        def _(b):
            attend(k, b)

        @pl.loop(0, step)
        def _(i):
            c = k * step + i
            gathered[c, place, side] = jnp.concatenate(
                [
                    heads[k, pl.ds(i * per_chunk + j, rows, stride=group), :]
                    for j in range(per_chunk)
                ],
                axis=1,
            ).astype(jnp.bfloat16)
            for d in range(1, pairs):
                ctx_far(c, d, place).start()

        @pl.when(k > 0)
        def _():
            @pl.loop(0, step)
            def _(i):
                forward((k - 1) * step + i)

    @pl.loop(0, step)
    def _(i):
        forward((stages - 1) * step + i)

    @pl.loop(0, query_chunks)
    def _(c):
        multiply(c)

    swap = remote(acc.at[1 - half], across, tp_sem.at[0], tp_sem.at[1], other_core)
    swap.start()

    @pl.loop(0, chunks)
    def _(c):
        near(c).wait_send()
        for d in range(1, pairs):
            far(c, d).wait_send()

    @pl.loop(0, query_chunks)
    def _(c):
        ctx_near(c, side).wait_send()
        for d in range(1, pairs):
            ctx_far(c, d, place).wait_send()

    for g in range(2):
        near_stat(g).wait_send()
        for d in range(1, pairs):
            far_stat(g, d).wait_send()
    swap.wait()
    out[...] = (acc[half] + across[...]).astype(jnp.bfloat16)


def local(
    tokens,
    gain,
    w_query,
    w_key,
    w_value,
    bias_query,
    bias_key,
    bias_value,
    w_output,
    cache_keys,
    cache_values,
    lengths,
    request_of_slot,
):
    pairs = lax.axis_size("pool") // 2
    total_rows, depth = tokens.shape
    count = total_rows // 2
    rows = count // pairs
    width = w_key.shape[1]
    query_chunks = w_query.shape[1] // width
    chunks = query_chunks + 2
    head_count = w_query.shape[1] // HD
    span = cache_keys.shape[1]
    columns = w_output.shape[1]
    stages = width // HD
    vmem = pl.BlockSpec(memory_space=pltpu.VMEM)
    hbm = pl.BlockSpec(memory_space=pl.ANY)
    dma = pltpu.SemaphoreType.DMA
    bf16, f32, i16 = jnp.bfloat16, jnp.float32, jnp.int16
    return pl.pallas_call(
        functools.partial(layer_kernel, pairs),
        out_shape=jax.ShapeDtypeStruct((count, columns), bf16),
        in_specs=[pl.BlockSpec(memory_space=pltpu.SMEM)] + [vmem] * 7 + [hbm] * 6,
        out_specs=vmem,
        scratch_shapes=[
            pltpu.VMEM((chunks, depth, width), bf16),
            pltpu.VMEM((total_rows, total_rows), bf16),
            pltpu.VMEM((pairs, 2, rows, depth), bf16),
            pltpu.VMEM((pairs, 2, rows, HD), f32),
            pltpu.VMEM((chunks, pairs, rows, width), f32),
            pltpu.VMEM((chunks, pairs, rows, width), i16),
            pltpu.VMEM((chunks, pairs, rows, width), i16),
            pltpu.VMEM((chunks, pairs - 1, rows, width), i16),
            pltpu.VMEM((2, count, HD), f32),
            pltpu.VMEM((2, count, HD), f32),
            pltpu.VMEM((2, pairs, rows, HD), f32),
            pltpu.VMEM((2, pairs - 1, rows, HD), f32),
            pltpu.VMEM((rows, span, width), bf16),
            pltpu.VMEM((rows, span, width), bf16),
            pltpu.VMEM((stages, rows * head_count // stages, HD), f32),
            pltpu.VMEM((3, rows, HD), f32),
            pltpu.VMEM((stages, rows, HD), f32),
            pltpu.VMEM((stages, rows, HD), f32),
            pltpu.VMEM((query_chunks, width, columns), bf16),
            pltpu.VMEM((query_chunks, pairs, 2, rows, width), bf16),
            pltpu.VMEM((2, count, columns), f32),
            pltpu.VMEM((count, columns), f32),
            dma((chunks,)),
            dma((chunks,)),
            dma((chunks,)),
            dma((chunks, pairs - 1)),
            dma((chunks, pairs - 1)),
            dma((2, 2)),
            dma((2, pairs - 1)),
            dma((2, pairs - 1)),
            dma((2,)),
            dma((query_chunks,)),
            dma((query_chunks, pairs - 1)),
            dma((query_chunks, pairs - 1)),
            dma((query_chunks,)),
            dma((query_chunks,)),
            dma((2,)),
        ],
        compiler_params=pltpu.CompilerParams(
            collective_id=0, has_side_effects=True, vmem_limit_bytes=62 * MIB
        ),
        cost_estimate=pl.CostEstimate(
            flops=4 * total_rows * depth * chunks * width,
            bytes_accessed=2 * depth * chunks * width + 4 * rows * span * width,
            transcendentals=rows * head_count * span,
        ),
    )(
        lengths,
        lengths[None, :],
        request_of_slot[None, :],
        tokens,
        gain[None, :],
        bias_query[None, :],
        bias_key[None, :],
        bias_value[None, :],
        w_query,
        w_key,
        w_value,
        w_output,
        cache_keys,
        cache_values,
    )


def solution(mesh):
    in_specs = (
        P("groups", "pool"),
        P("pool"),
        P("pool", "tp"),
        P("pool", "tp"),
        P("pool", "tp"),
        P("tp"),
        P("tp"),
        P("tp"),
        P("tp", "pool"),
        P(("groups", "pool"), None, "tp"),
        P(("groups", "pool"), None, "tp"),
        P(("groups", "pool")),
        P("groups"),
    )
    out_specs = P(("groups", "tp"), "pool")
    return jax.shard_map(local, mesh=mesh, in_specs=in_specs, out_specs=out_specs, check_vma=False)
```

```python
import functools
import math
import jax
import jax.numpy as jnp
from jax import lax
from jax.experimental import pallas as pl
from jax.experimental.pallas import tpu as pltpu
from jax.sharding import PartitionSpec as P

D = 8192
HD = 128


ROPE_BASE = 1000000.0
EPSILON = 1e-06
NEGATIVE = -1e30
MIB = 1 << 20
LEVELS = 32000.0


def greet(devices):
    barrier = pltpu.get_barrier_semaphore()
    for device in devices:
        pl.semaphore_signal(
            barrier, inc=1, device_id=device, device_id_type=pl.DeviceIdType.MESH
        )
    pl.semaphore_wait(barrier, len(devices))


def remote(src, dst, send, recv, device):
    return pltpu.make_async_remote_copy(
        src_ref=src,
        dst_ref=dst,
        send_sem=send,
        recv_sem=recv,
        device_id=device,
        device_id_type=pl.DeviceIdType.MESH,
    )


def lane(stats, c):
    index = lax.broadcasted_iota(jnp.int32, stats.shape, 1)
    return jnp.sum(jnp.where(index == c, stats, 0.0), axis=1, keepdims=True)


def with_lane(stats, c, column):
    index = lax.broadcasted_iota(jnp.int32, stats.shape, 1)
    return jnp.where(index == c, column, stats)


def encode(values, bound):
    factor = jnp.where(bound > 1e-30, LEVELS / jnp.maximum(bound, 1e-30), 0.0)
    return jnp.round(values * factor).astype(jnp.int32).astype(jnp.int16)


def decode(codes, bound):
    return codes.astype(jnp.int32).astype(jnp.float32) * (bound * (1.0 / LEVELS))


def layer_kernel(
    pairs,
    lengths,
    lengths_row,
    slots,
    tokens,
    gain,
    bias_query,
    bias_key,
    bias_value,
    w_query,
    w_key,
    w_value,
    w_output,
    cache_keys,
    cache_values,
    out,
    weights,
    chosen,
    x,
    squares,
    mine,
    near_out,
    near_in,
    far_in,
    near_stat_out,
    near_stat_in,
    stat_sum,
    far_stat_in,
    keys,
    values,
    heads,
    turns,
    key_new,
    value_new,
    out_weights,
    gathered,
    acc,
    across,
    w_sem,
    near_send,
    near_recv,
    far_send,
    far_recv,
    stat_sem,
    far_stat_send,
    far_stat_recv,
    cache_sem,
    out_w_sem,
    ctx_far_send,
    ctx_far_recv,
    ctx_near_send,
    ctx_near_recv,
    tp_sem,
):
    me = lax.axis_index("pool")
    half = lax.axis_index("tp")
    place, side = me // 2, me % 2
    chunks, depth, width = weights.shape
    query_chunks = chunks - 2
    _, _, rows, _ = mine.shape
    count = pairs * rows
    total_rows = 2 * count
    per_chunk = width // HD
    stages, per_stage, _ = heads.shape
    group = per_stage // rows
    step = query_chunks // stages
    first = 2 + step
    span = keys.shape[1]
    batch = 8
    partner = {"pool": place * 2 + 1 - side}
    other_core = {"tp": 1 - half}
    peers = [{"pool": lax.rem(place + d, pairs) * 2 + side} for d in range(1, pairs)]

    def query_load(c):
        columns = pl.ds(pl.multiple_of((c - 2) * width, width), width)
        return pltpu.make_async_copy(w_query.at[:, columns], weights.at[c], w_sem.at[c])

    def out_load(c):
        part = pl.ds(pl.multiple_of(c * width, width), width)
        return pltpu.make_async_copy(w_output.at[part, :], out_weights.at[c], out_w_sem.at[c])

    def near(c):
        return remote(
            near_out.at[c], near_in.at[c], near_send.at[c], near_recv.at[c], partner
        )

    def near_stat(g):
        return remote(
            near_stat_out.at[g], near_stat_in.at[g], stat_sem.at[0, g], stat_sem.at[1, g], partner
        )

    def far(c, d):
        return remote(
            near_in.at[c, lax.rem(place + d, pairs)],
            far_in.at[c, d - 1],
            far_send.at[c, d - 1],
            far_recv.at[c, d - 1],
            peers[d - 1],
        )

    def far_stat(g, d):
        return remote(
            stat_sum.at[g, lax.rem(place + d, pairs)],
            far_stat_in.at[g, d - 1],
            far_stat_send.at[g, d - 1],
            far_stat_recv.at[g, d - 1],
            peers[d - 1],
        )

    def ctx_far(c, d, source):
        slot = gathered.at[c, source, side]
        return remote(
            slot, slot, ctx_far_send.at[c, d - 1], ctx_far_recv.at[c, d - 1], peers[d - 1]
        )

    def ctx_near(c, source, which):
        slot = gathered.at[c, source, which]
        return remote(
            slot, slot, ctx_near_send.at[c, source], ctx_near_recv.at[c, source], partner
        )

    key_load = pltpu.make_async_copy(w_key, weights.at[0], w_sem.at[0])
    value_load = pltpu.make_async_copy(w_value, weights.at[1], w_sem.at[1])
    key_load.start()
    value_load.start()

    @pl.loop(2, chunks)
    def _(c):
        query_load(c).start()

    requests = lax.broadcasted_iota(jnp.int32, (total_rows, total_rows), 0)
    chosen[...] = jnp.where(requests == slots[...], 1.0, 0.0).astype(jnp.bfloat16)
    ordered = lax.dot_general(
        chosen[...], tokens[...], (((0,), (0,)), ((), ())), preferred_element_type=jnp.float32
    )
    square = jnp.sum(ordered * ordered, axis=1, keepdims=True)
    squares[...] = jnp.broadcast_to(square, (total_rows, HD)).reshape(squares.shape)
    x[...] = (ordered * gain[...]).astype(jnp.bfloat16).reshape(x.shape)
    greet([partner, other_core] + peers)

    for g, start, stop in ((0, 0, first), (1, first, chunks)):
        near_stat_out[g] = squares[:, 1 - side].reshape(count, HD)

        @pl.loop(start, stop)
        def _(c):
            pltpu.make_async_copy(weights.at[c], weights.at[c], w_sem.at[c]).wait()
            part = jnp.dot(
                x[:, 1 - side].reshape(count, depth),
                weights[c],
                preferred_element_type=jnp.float32,
            )
            bound = jnp.max(jnp.abs(part), axis=1, keepdims=True)
            near_stat_out[g] = with_lane(near_stat_out[g], c, bound)
            near_out[c] = encode(part, bound).reshape(pairs, rows, width)

        near_stat(g).start()

        @pl.loop(start, stop)
        def _(c):
            near(c).start()

    key_cache_load = pltpu.make_async_copy(cache_keys, keys, cache_sem.at[0])
    value_cache_load = pltpu.make_async_copy(cache_values, values, cache_sem.at[1])
    key_cache_load.start()
    value_cache_load.start()

    @pl.loop(0, query_chunks)
    def _(c):
        out_load(c).start()

    def keep(g, start, stop):
        stat_sum[g] = squares[:, side]

        @pl.loop(start, stop)
        def _(c):
            part = jnp.dot(
                x[:, side].reshape(count, depth), weights[c], preferred_element_type=jnp.float32
            )
            bound = jnp.max(jnp.abs(part), axis=1, keepdims=True)
            stat_sum[g] = with_lane(stat_sum[g].reshape(count, HD), c, bound).reshape(
                pairs, rows, HD
            )
            mine[c] = part.reshape(pairs, rows, width)

    def bounds(g):
        near_stat(g).wait_recv()
        stat_sum[g] = stat_sum[g] + near_stat_in[g].reshape(pairs, rows, HD)
        for d in range(1, pairs):
            far_stat(g, d).start()

    def middle(g, c):
        near(c).wait_recv()
        both = mine[c].reshape(count, width) + decode(
            near_in[c].reshape(count, width), lane(near_stat_in[g], c)
        )
        mine[c] = both.reshape(pairs, rows, width)
        bound = lane(stat_sum[g].reshape(count, HD), c)
        near_in[c] = encode(both, bound).reshape(pairs, rows, width)
        for d in range(1, pairs):
            far(c, d).start()

    keep(0, 0, first)
    bounds(0)

    @pl.loop(0, first)
    def _(c):
        middle(0, c)

    keep(1, first, chunks)
    bounds(1)

    here = lax.broadcasted_iota(jnp.int32, (rows, rows), 0)
    there = lax.broadcasted_iota(jnp.int32, (rows, rows), 1)
    length = jnp.sum(
        jnp.where(here == there, lengths_row[...].astype(jnp.float32), 0.0), axis=1, keepdims=True
    )
    index = lax.broadcasted_iota(jnp.int32, (rows, HD), 1)
    index = jnp.where(index < HD // 2, index, index - HD // 2).astype(jnp.float32)
    angles = length * jnp.exp(index * (-2.0 * math.log(ROPE_BASE) / HD))
    sign = jnp.where(lax.broadcasted_iota(jnp.int32, (rows, HD), 1) < HD // 2, -1.0, 1.0)
    turns[0] = jnp.cos(angles)
    turns[1] = jnp.sin(angles) * sign

    square_sum = lane(stat_sum[0, place], HD - 1)
    for d in range(1, pairs):
        far_stat(0, d).wait_recv()
        square_sum = square_sum + lane(far_stat_in[0, d - 1], HD - 1)
    turns[2] = jnp.broadcast_to(
        1.0 / jnp.sqrt(square_sum / (depth * pairs * 2) + EPSILON), (rows, HD)
    )

    def finish(g, c, bias):
        total = mine[c, place]
        for d in range(1, pairs):
            far(c, d).wait_recv()
            total = total + decode(far_in[c, d - 1], lane(far_stat_in[g, d - 1], c))
        return total * turns[2, :, 0:1] + bias

    def turned(vectors, j):
        one = vectors[:, j * HD : (j + 1) * HD]
        return one * turns[0] + pltpu.roll(one, HD // 2, 1) * turns[1]

    key = finish(0, 0, bias_key[...])
    for j in range(stages):
        key_new[j] = turned(key, j).astype(jnp.bfloat16).astype(jnp.float32)
    value = finish(0, 1, bias_value[...])
    for j in range(stages):
        value_new[j] = value[:, j * HD : (j + 1) * HD].astype(jnp.bfloat16).astype(jnp.float32)

    position = lax.broadcasted_iota(jnp.int32, (group, span), 1)
    scaling = HD ** (-0.5)

    def repeated(ref, k, n):
        return jnp.concatenate(
            [jnp.broadcast_to(ref[k, pl.ds(n + j, 1), :], (group, HD)) for j in range(batch)],
            axis=0,
        )

    def attend(k, b):
        n = b * batch
        columns = pl.ds(pl.multiple_of(k * HD, HD), HD)
        own = pl.ds(pl.multiple_of(n * group, batch * group), batch * group)
        query = heads[k, own, :].astype(jnp.bfloat16).astype(jnp.float32)
        scores = []
        for j in range(batch):
            score = lax.dot_general(
                query[j * group : (j + 1) * group].astype(jnp.bfloat16),
                keys[n + j, :, columns],
                (((1,), (1,)), ((), ())),
                preferred_element_type=jnp.float32,
            )
            scores.append(jnp.where(position < lengths[n + j], score * scaling, NEGATIVE))
        older = jnp.concatenate(scores, axis=0)
        newest = jnp.sum(query * repeated(key_new, k, n), axis=1, keepdims=True) * scaling
        highest = jnp.maximum(jnp.max(older, axis=1, keepdims=True), newest)
        w_old = jnp.exp(older - highest)
        w_new = jnp.exp(newest - highest)
        denominator = jnp.sum(w_old, axis=1, keepdims=True) + w_new
        p_old = w_old / denominator
        p_new = (w_new / denominator).astype(jnp.bfloat16).astype(jnp.float32)
        context = jnp.concatenate(
            [
                jnp.dot(
                    p_old[j * group : (j + 1) * group].astype(jnp.bfloat16),
                    values[n + j, :, columns],
                    preferred_element_type=jnp.float32,
                )
                for j in range(batch)
            ],
            axis=0,
        )
        heads[k, own, :] = context + p_new * repeated(value_new, k, n)

    def forward(c):
        for d in range(1, pairs):
            source = lax.rem(place + pairs - d, pairs)
            ctx_far(c, d, source).wait_recv()
            ctx_near(c, source, side).start()

    acc[...] = jnp.zeros_like(acc)

    def multiply(c):
        for source in range(pairs):
            ctx_near(c, source, 1 - side).wait_recv()
        out_load(c).wait()
        by_request = jnp.dot(
            chosen[...],
            gathered[c].reshape(total_rows, width),
            preferred_element_type=jnp.float32,
        ).astype(jnp.bfloat16)
        acc[...] += jnp.dot(
            by_request, out_weights[c], preferred_element_type=jnp.float32
        ).reshape(acc.shape)

    key_cache_load.wait()
    value_cache_load.wait()

    @pl.loop(0, stages)
    def _(k):
        @pl.when(k < stages - 1)
        def _():
            @pl.loop(0, step)
            def _(i):
                middle(1, first + k * step + i)

        @pl.when(k == 1)
        def _():
            for d in range(1, pairs):
                far_stat(1, d).wait_recv()

        g = (k + stages - 2) // (stages - 1)

        @pl.loop(0, step)
        def _(i):
            c = k * step + i
            columns = pl.ds(pl.multiple_of(c * width, width), width)
            query = finish(g, 2 + c, bias_query[:, columns])
            for j in range(per_chunk):
                heads[k, pl.ds(i * per_chunk + j, rows, stride=group), :] = turned(query, j)

        @pl.loop(0, rows // batch)
        def _(b):
            attend(k, b)

        @pl.loop(0, step)
        def _(i):
            c = k * step + i
            gathered[c, place, side] = jnp.concatenate(
                [
                    heads[k, pl.ds(i * per_chunk + j, rows, stride=group), :]
                    for j in range(per_chunk)
                ],
                axis=1,
            ).astype(jnp.bfloat16)
            for d in range(1, pairs):
                ctx_far(c, d, place).start()
            ctx_near(c, place, side).start()

        @pl.when(k > 0)
        def _():
            @pl.loop(0, step)
            def _(i):
                forward((k - 1) * step + i)

    @pl.loop(0, step)
    def _(i):
        forward((stages - 1) * step + i)

    @pl.loop(0, query_chunks)
    def _(c):
        multiply(c)

    swap = remote(acc.at[1 - half], across, tp_sem.at[0], tp_sem.at[1], other_core)
    swap.start()

    @pl.loop(0, chunks)
    def _(c):
        near(c).wait_send()
        for d in range(1, pairs):
            far(c, d).wait_send()

    @pl.loop(0, query_chunks)
    def _(c):
        for source in range(pairs):
            ctx_near(c, source, side).wait_send()
        for d in range(1, pairs):
            ctx_far(c, d, place).wait_send()

    for g in range(2):
        near_stat(g).wait_send()
        for d in range(1, pairs):
            far_stat(g, d).wait_send()
    swap.wait()
    out[...] = (acc[half] + across[...]).astype(jnp.bfloat16)


def local(
    tokens,
    gain,
    w_query,
    w_key,
    w_value,
    bias_query,
    bias_key,
    bias_value,
    w_output,
    cache_keys,
    cache_values,
    lengths,
    request_of_slot,
):
    pairs = lax.axis_size("pool") // 2
    total_rows, depth = tokens.shape
    count = total_rows // 2
    rows = count // pairs
    width = w_key.shape[1]
    query_chunks = w_query.shape[1] // width
    chunks = query_chunks + 2
    head_count = w_query.shape[1] // HD
    span = cache_keys.shape[1]
    columns = w_output.shape[1]
    stages = width // HD
    vmem = pl.BlockSpec(memory_space=pltpu.VMEM)
    hbm = pl.BlockSpec(memory_space=pl.ANY)
    dma = pltpu.SemaphoreType.DMA
    bf16, f32, i16 = jnp.bfloat16, jnp.float32, jnp.int16
    return pl.pallas_call(
        functools.partial(layer_kernel, pairs),
        out_shape=jax.ShapeDtypeStruct((count, columns), bf16),
        in_specs=[pl.BlockSpec(memory_space=pltpu.SMEM)] + [vmem] * 7 + [hbm] * 6,
        out_specs=vmem,
        scratch_shapes=[
            pltpu.VMEM((chunks, depth, width), bf16),
            pltpu.VMEM((total_rows, total_rows), bf16),
            pltpu.VMEM((pairs, 2, rows, depth), bf16),
            pltpu.VMEM((pairs, 2, rows, HD), f32),
            pltpu.VMEM((chunks, pairs, rows, width), f32),
            pltpu.VMEM((chunks, pairs, rows, width), i16),
            pltpu.VMEM((chunks, pairs, rows, width), i16),
            pltpu.VMEM((chunks, pairs - 1, rows, width), i16),
            pltpu.VMEM((2, count, HD), f32),
            pltpu.VMEM((2, count, HD), f32),
            pltpu.VMEM((2, pairs, rows, HD), f32),
            pltpu.VMEM((2, pairs - 1, rows, HD), f32),
            pltpu.VMEM((rows, span, width), bf16),
            pltpu.VMEM((rows, span, width), bf16),
            pltpu.VMEM((stages, rows * head_count // stages, HD), f32),
            pltpu.VMEM((3, rows, HD), f32),
            pltpu.VMEM((stages, rows, HD), f32),
            pltpu.VMEM((stages, rows, HD), f32),
            pltpu.VMEM((query_chunks, width, columns), bf16),
            pltpu.VMEM((query_chunks, pairs, 2, rows, width), bf16),
            pltpu.VMEM((2, count, columns), f32),
            pltpu.VMEM((count, columns), f32),
            dma((chunks,)),
            dma((chunks,)),
            dma((chunks,)),
            dma((chunks, pairs - 1)),
            dma((chunks, pairs - 1)),
            dma((2, 2)),
            dma((2, pairs - 1)),
            dma((2, pairs - 1)),
            dma((2,)),
            dma((query_chunks,)),
            dma((query_chunks, pairs - 1)),
            dma((query_chunks, pairs - 1)),
            dma((query_chunks, pairs)),
            dma((query_chunks, pairs)),
            dma((2,)),
        ],
        compiler_params=pltpu.CompilerParams(
            collective_id=0, has_side_effects=True, vmem_limit_bytes=62 * MIB
        ),
        cost_estimate=pl.CostEstimate(
            flops=4 * total_rows * depth * chunks * width,
            bytes_accessed=2 * depth * chunks * width + 4 * rows * span * width,
            transcendentals=rows * head_count * span,
        ),
    )(
        lengths,
        lengths[None, :],
        request_of_slot[None, :],
        tokens,
        gain[None, :],
        bias_query[None, :],
        bias_key[None, :],
        bias_value[None, :],
        w_query,
        w_key,
        w_value,
        w_output,
        cache_keys,
        cache_values,
    )


def solution(mesh):
    in_specs = (
        P("groups", "pool"),
        P("pool"),
        P("pool", "tp"),
        P("pool", "tp"),
        P("pool", "tp"),
        P("tp"),
        P("tp"),
        P("tp"),
        P("tp", "pool"),
        P(("groups", "pool"), None, "tp"),
        P(("groups", "pool"), None, "tp"),
        P(("groups", "pool")),
        P("groups"),
    )
    out_specs = P(("groups", "tp"), "pool")
    return jax.shard_map(local, mesh=mesh, in_specs=in_specs, out_specs=out_specs, check_vma=False)
```

```python
import functools
import math
import jax
import jax.numpy as jnp
from jax import lax
from jax.experimental import pallas as pl
from jax.experimental.pallas import tpu as pltpu
from jax.sharding import PartitionSpec as P

D = 8192
HD = 128


ROPE_BASE = 1000000.0
EPSILON = 1e-06
NEGATIVE = -1e30
MIB = 1 << 20
LEVELS = 32000.0


def greet(devices):
    barrier = pltpu.get_barrier_semaphore()
    for device in devices:
        pl.semaphore_signal(
            barrier, inc=1, device_id=device, device_id_type=pl.DeviceIdType.MESH
        )
    pl.semaphore_wait(barrier, len(devices))


def remote(src, dst, send, recv, device):
    return pltpu.make_async_remote_copy(
        src_ref=src,
        dst_ref=dst,
        send_sem=send,
        recv_sem=recv,
        device_id=device,
        device_id_type=pl.DeviceIdType.MESH,
    )


def lane(stats, c):
    index = lax.broadcasted_iota(jnp.int32, stats.shape, 1)
    return jnp.sum(jnp.where(index == c, stats, 0.0), axis=1, keepdims=True)


def with_lane(stats, c, column):
    index = lax.broadcasted_iota(jnp.int32, stats.shape, 1)
    return jnp.where(index == c, column, stats)


def encode(values, bound):
    factor = jnp.where(bound > 1e-30, LEVELS / jnp.maximum(bound, 1e-30), 0.0)
    return jnp.round(values * factor).astype(jnp.int32).astype(jnp.int16)


def decode(codes, bound):
    return codes.astype(jnp.int32).astype(jnp.float32) * (bound * (1.0 / LEVELS))


def layer_kernel(
    pairs,
    lengths,
    lengths_row,
    slots,
    tokens,
    gain,
    bias_query,
    bias_key,
    bias_value,
    w_query,
    w_key,
    w_value,
    w_output,
    cache_keys,
    cache_values,
    out,
    weights,
    chosen,
    x,
    squares,
    mine,
    near_out,
    near_in,
    far_in,
    near_stat_out,
    near_stat_in,
    stat_sum,
    far_stat_in,
    keys,
    values,
    heads,
    turns,
    key_new,
    value_new,
    out_weights,
    gathered,
    acc,
    across,
    w_sem,
    near_send,
    near_recv,
    far_send,
    far_recv,
    stat_sem,
    far_stat_send,
    far_stat_recv,
    cache_sem,
    out_w_sem,
    ctx_far_send,
    ctx_far_recv,
    ctx_near_send,
    ctx_near_recv,
    tp_sem,
):
    me = lax.axis_index("pool")
    half = lax.axis_index("tp")
    place, side = me // 2, me % 2
    chunks, depth, width = weights.shape
    query_chunks = chunks - 2
    _, _, rows, _ = mine.shape
    count = pairs * rows
    total_rows = 2 * count
    per_chunk = width // HD
    stages, per_stage, _ = heads.shape
    group = per_stage // rows
    step = query_chunks // stages
    first = 2 + step
    span = keys.shape[1]
    batch = 8
    partner = {"pool": place * 2 + 1 - side}
    other_core = {"tp": 1 - half}
    peers = [{"pool": lax.rem(place + d, pairs) * 2 + side} for d in range(1, pairs)]

    def query_load(c):
        columns = pl.ds(pl.multiple_of((c - 2) * width, width), width)
        return pltpu.make_async_copy(w_query.at[:, columns], weights.at[c], w_sem.at[c])

    def out_load(c):
        part = pl.ds(pl.multiple_of(c * width, width), width)
        return pltpu.make_async_copy(w_output.at[part, :], out_weights.at[c], out_w_sem.at[c])

    def near(c):
        return remote(
            near_out.at[c], near_in.at[c], near_send.at[c], near_recv.at[c], partner
        )

    def near_stat(g):
        return remote(
            near_stat_out.at[g], near_stat_in.at[g], stat_sem.at[0, g], stat_sem.at[1, g], partner
        )

    def far(c, d):
        return remote(
            near_in.at[c, lax.rem(place + d, pairs)],
            far_in.at[c, d - 1],
            far_send.at[c, d - 1],
            far_recv.at[c, d - 1],
            peers[d - 1],
        )

    def far_stat(g, d):
        return remote(
            stat_sum.at[g, lax.rem(place + d, pairs)],
            far_stat_in.at[g, d - 1],
            far_stat_send.at[g, d - 1],
            far_stat_recv.at[g, d - 1],
            peers[d - 1],
        )

    ways = ((0, 1), (1, -1))

    def inside(at):
        return (at >= 0) & (at < pairs)

    def ctx_far(c, source, target, index):
        slot = gathered.at[c, source, side]
        return remote(
            slot,
            slot,
            ctx_far_send.at[c, index],
            ctx_far_recv.at[c, source],
            {"pool": target * 2 + side},
        )

    def ctx_near(c, source, which):
        slot = gathered.at[c, source, which]
        return remote(
            slot, slot, ctx_near_send.at[c, source], ctx_near_recv.at[c, source], partner
        )

    key_load = pltpu.make_async_copy(w_key, weights.at[0], w_sem.at[0])
    value_load = pltpu.make_async_copy(w_value, weights.at[1], w_sem.at[1])
    key_load.start()
    value_load.start()

    @pl.loop(2, chunks)
    def _(c):
        query_load(c).start()

    requests = lax.broadcasted_iota(jnp.int32, (total_rows, total_rows), 0)
    chosen[...] = jnp.where(requests == slots[...], 1.0, 0.0).astype(jnp.bfloat16)
    ordered = lax.dot_general(
        chosen[...], tokens[...], (((0,), (0,)), ((), ())), preferred_element_type=jnp.float32
    )
    square = jnp.sum(ordered * ordered, axis=1, keepdims=True)
    squares[...] = jnp.broadcast_to(square, (total_rows, HD)).reshape(squares.shape)
    x[...] = (ordered * gain[...]).astype(jnp.bfloat16).reshape(x.shape)
    greet([partner, other_core] + peers)

    for g, start, stop in ((0, 0, first), (1, first, chunks)):
        near_stat_out[g] = squares[:, 1 - side].reshape(count, HD)

        @pl.loop(start, stop)
        def _(c):
            pltpu.make_async_copy(weights.at[c], weights.at[c], w_sem.at[c]).wait()
            part = jnp.dot(
                x[:, 1 - side].reshape(count, depth),
                weights[c],
                preferred_element_type=jnp.float32,
            )
            bound = jnp.max(jnp.abs(part), axis=1, keepdims=True)
            near_stat_out[g] = with_lane(near_stat_out[g], c, bound)
            near_out[c] = encode(part, bound).reshape(pairs, rows, width)

        near_stat(g).start()

        @pl.loop(start, stop)
        def _(c):
            near(c).start()

    key_cache_load = pltpu.make_async_copy(cache_keys, keys, cache_sem.at[0])
    value_cache_load = pltpu.make_async_copy(cache_values, values, cache_sem.at[1])
    key_cache_load.start()
    value_cache_load.start()

    @pl.loop(0, query_chunks)
    def _(c):
        out_load(c).start()

    def keep(g, start, stop):
        stat_sum[g] = squares[:, side]

        @pl.loop(start, stop)
        def _(c):
            part = jnp.dot(
                x[:, side].reshape(count, depth), weights[c], preferred_element_type=jnp.float32
            )
            bound = jnp.max(jnp.abs(part), axis=1, keepdims=True)
            stat_sum[g] = with_lane(stat_sum[g].reshape(count, HD), c, bound).reshape(
                pairs, rows, HD
            )
            mine[c] = part.reshape(pairs, rows, width)

    def bounds(g):
        near_stat(g).wait_recv()
        stat_sum[g] = stat_sum[g] + near_stat_in[g].reshape(pairs, rows, HD)
        for d in range(1, pairs):
            far_stat(g, d).start()

    def middle(g, c):
        near(c).wait_recv()
        both = mine[c].reshape(count, width) + decode(
            near_in[c].reshape(count, width), lane(near_stat_in[g], c)
        )
        mine[c] = both.reshape(pairs, rows, width)
        bound = lane(stat_sum[g].reshape(count, HD), c)
        near_in[c] = encode(both, bound).reshape(pairs, rows, width)
        for d in range(1, pairs):
            far(c, d).start()

    keep(0, 0, first)
    bounds(0)

    @pl.loop(0, first)
    def _(c):
        middle(0, c)

    keep(1, first, chunks)
    bounds(1)

    here = lax.broadcasted_iota(jnp.int32, (rows, rows), 0)
    there = lax.broadcasted_iota(jnp.int32, (rows, rows), 1)
    length = jnp.sum(
        jnp.where(here == there, lengths_row[...].astype(jnp.float32), 0.0), axis=1, keepdims=True
    )
    index = lax.broadcasted_iota(jnp.int32, (rows, HD), 1)
    index = jnp.where(index < HD // 2, index, index - HD // 2).astype(jnp.float32)
    angles = length * jnp.exp(index * (-2.0 * math.log(ROPE_BASE) / HD))
    sign = jnp.where(lax.broadcasted_iota(jnp.int32, (rows, HD), 1) < HD // 2, -1.0, 1.0)
    turns[0] = jnp.cos(angles)
    turns[1] = jnp.sin(angles) * sign

    square_sum = lane(stat_sum[0, place], HD - 1)
    for d in range(1, pairs):
        far_stat(0, d).wait_recv()
        square_sum = square_sum + lane(far_stat_in[0, d - 1], HD - 1)
    turns[2] = jnp.broadcast_to(
        1.0 / jnp.sqrt(square_sum / (depth * pairs * 2) + EPSILON), (rows, HD)
    )

    def finish(g, c, bias):
        total = mine[c, place]
        for d in range(1, pairs):
            far(c, d).wait_recv()
            total = total + decode(far_in[c, d - 1], lane(far_stat_in[g, d - 1], c))
        return total * turns[2, :, 0:1] + bias

    def turned(vectors, j):
        one = vectors[:, j * HD : (j + 1) * HD]
        return one * turns[0] + pltpu.roll(one, HD // 2, 1) * turns[1]

    key = finish(0, 0, bias_key[...])
    for j in range(stages):
        key_new[j] = turned(key, j).astype(jnp.bfloat16).astype(jnp.float32)
    value = finish(0, 1, bias_value[...])
    for j in range(stages):
        value_new[j] = value[:, j * HD : (j + 1) * HD].astype(jnp.bfloat16).astype(jnp.float32)

    position = lax.broadcasted_iota(jnp.int32, (group, span), 1)
    scaling = HD ** (-0.5)

    def repeated(ref, k, n):
        return jnp.concatenate(
            [jnp.broadcast_to(ref[k, pl.ds(n + j, 1), :], (group, HD)) for j in range(batch)],
            axis=0,
        )

    def attend(k, b):
        n = b * batch
        columns = pl.ds(pl.multiple_of(k * HD, HD), HD)
        own = pl.ds(pl.multiple_of(n * group, batch * group), batch * group)
        query = heads[k, own, :].astype(jnp.bfloat16).astype(jnp.float32)
        scores = []
        for j in range(batch):
            score = lax.dot_general(
                query[j * group : (j + 1) * group].astype(jnp.bfloat16),
                keys[n + j, :, columns],
                (((1,), (1,)), ((), ())),
                preferred_element_type=jnp.float32,
            )
            scores.append(jnp.where(position < lengths[n + j], score * scaling, NEGATIVE))
        older = jnp.concatenate(scores, axis=0)
        newest = jnp.sum(query * repeated(key_new, k, n), axis=1, keepdims=True) * scaling
        highest = jnp.maximum(jnp.max(older, axis=1, keepdims=True), newest)
        w_old = jnp.exp(older - highest)
        w_new = jnp.exp(newest - highest)
        denominator = jnp.sum(w_old, axis=1, keepdims=True) + w_new
        p_old = w_old / denominator
        p_new = (w_new / denominator).astype(jnp.bfloat16).astype(jnp.float32)
        context = jnp.concatenate(
            [
                jnp.dot(
                    p_old[j * group : (j + 1) * group].astype(jnp.bfloat16),
                    values[n + j, :, columns],
                    preferred_element_type=jnp.float32,
                )
                for j in range(batch)
            ],
            axis=0,
        )
        heads[k, own, :] = context + p_new * repeated(value_new, k, n)

    def forward(c):
        for hops in range(1, pairs):
            for way, sign in ways:
                source = place - sign * hops

                @pl.when(inside(source))
                def _():
                    ctx_far(c, source, lax.rem(place + 1, pairs), 0).wait_recv()
                    if hops > 1:

                        @pl.when(inside(place + sign))
                        def _():
                            ctx_far(c, source, place + sign, 2 * hops + way).start()

                    ctx_near(c, source, side).start()

    acc[...] = jnp.zeros_like(acc)

    def multiply(c):
        for source in range(pairs):
            ctx_near(c, source, 1 - side).wait_recv()
        out_load(c).wait()
        by_request = jnp.dot(
            chosen[...],
            gathered[c].reshape(total_rows, width),
            preferred_element_type=jnp.float32,
        ).astype(jnp.bfloat16)
        acc[...] += jnp.dot(
            by_request, out_weights[c], preferred_element_type=jnp.float32
        ).reshape(acc.shape)

    key_cache_load.wait()
    value_cache_load.wait()

    @pl.loop(0, stages)
    def _(k):
        @pl.when(k < stages - 1)
        def _():
            @pl.loop(0, step)
            def _(i):
                middle(1, first + k * step + i)

        @pl.when(k == 1)
        def _():
            for d in range(1, pairs):
                far_stat(1, d).wait_recv()

        g = (k + stages - 2) // (stages - 1)

        @pl.loop(0, step)
        def _(i):
            c = k * step + i
            columns = pl.ds(pl.multiple_of(c * width, width), width)
            query = finish(g, 2 + c, bias_query[:, columns])
            for j in range(per_chunk):
                heads[k, pl.ds(i * per_chunk + j, rows, stride=group), :] = turned(query, j)

        @pl.loop(0, rows // batch)
        def _(b):
            attend(k, b)

        @pl.loop(0, step)
        def _(i):
            c = k * step + i
            gathered[c, place, side] = jnp.concatenate(
                [
                    heads[k, pl.ds(i * per_chunk + j, rows, stride=group), :]
                    for j in range(per_chunk)
                ],
                axis=1,
            ).astype(jnp.bfloat16)
            for hops in (1, 2):
                for way, sign in ways:

                    @pl.when(inside(place + sign * hops))
                    def _():
                        ctx_far(c, place, place + sign * hops, 2 * hops - 2 + way).start()

            ctx_near(c, place, side).start()

        @pl.when(k > 0)
        def _():
            @pl.loop(0, step)
            def _(i):
                forward((k - 1) * step + i)

    @pl.loop(0, step)
    def _(i):
        forward((stages - 1) * step + i)

    @pl.loop(0, query_chunks)
    def _(c):
        multiply(c)

    swap = remote(acc.at[1 - half], across, tp_sem.at[0], tp_sem.at[1], other_core)
    swap.start()

    @pl.loop(0, chunks)
    def _(c):
        near(c).wait_send()
        for d in range(1, pairs):
            far(c, d).wait_send()

    @pl.loop(0, query_chunks)
    def _(c):
        for source in range(pairs):
            ctx_near(c, source, side).wait_send()
        for hops in (1, 2):
            for way, sign in ways:

                @pl.when(inside(place + sign * hops))
                def _():
                    ctx_far(c, place, place + sign * hops, 2 * hops - 2 + way).wait_send()

        for hops in range(2, pairs):
            for way, sign in ways:

                @pl.when(inside(place - sign * hops) & inside(place + sign))
                def _():
                    ctx_far(c, place - sign * hops, place + sign, 2 * hops + way).wait_send()


    for g in range(2):
        near_stat(g).wait_send()
        for d in range(1, pairs):
            far_stat(g, d).wait_send()
    swap.wait()
    out[...] = (acc[half] + across[...]).astype(jnp.bfloat16)


def local(
    tokens,
    gain,
    w_query,
    w_key,
    w_value,
    bias_query,
    bias_key,
    bias_value,
    w_output,
    cache_keys,
    cache_values,
    lengths,
    request_of_slot,
):
    pairs = lax.axis_size("pool") // 2
    total_rows, depth = tokens.shape
    count = total_rows // 2
    rows = count // pairs
    width = w_key.shape[1]
    query_chunks = w_query.shape[1] // width
    chunks = query_chunks + 2
    head_count = w_query.shape[1] // HD
    span = cache_keys.shape[1]
    columns = w_output.shape[1]
    stages = width // HD
    vmem = pl.BlockSpec(memory_space=pltpu.VMEM)
    hbm = pl.BlockSpec(memory_space=pl.ANY)
    dma = pltpu.SemaphoreType.DMA
    bf16, f32, i16 = jnp.bfloat16, jnp.float32, jnp.int16
    return pl.pallas_call(
        functools.partial(layer_kernel, pairs),
        out_shape=jax.ShapeDtypeStruct((count, columns), bf16),
        in_specs=[pl.BlockSpec(memory_space=pltpu.SMEM)] + [vmem] * 7 + [hbm] * 6,
        out_specs=vmem,
        scratch_shapes=[
            pltpu.VMEM((chunks, depth, width), bf16),
            pltpu.VMEM((total_rows, total_rows), bf16),
            pltpu.VMEM((pairs, 2, rows, depth), bf16),
            pltpu.VMEM((pairs, 2, rows, HD), f32),
            pltpu.VMEM((chunks, pairs, rows, width), f32),
            pltpu.VMEM((chunks, pairs, rows, width), i16),
            pltpu.VMEM((chunks, pairs, rows, width), i16),
            pltpu.VMEM((chunks, pairs - 1, rows, width), i16),
            pltpu.VMEM((2, count, HD), f32),
            pltpu.VMEM((2, count, HD), f32),
            pltpu.VMEM((2, pairs, rows, HD), f32),
            pltpu.VMEM((2, pairs - 1, rows, HD), f32),
            pltpu.VMEM((rows, span, width), bf16),
            pltpu.VMEM((rows, span, width), bf16),
            pltpu.VMEM((stages, rows * head_count // stages, HD), f32),
            pltpu.VMEM((3, rows, HD), f32),
            pltpu.VMEM((stages, rows, HD), f32),
            pltpu.VMEM((stages, rows, HD), f32),
            pltpu.VMEM((query_chunks, width, columns), bf16),
            pltpu.VMEM((query_chunks, pairs, 2, rows, width), bf16),
            pltpu.VMEM((2, count, columns), f32),
            pltpu.VMEM((count, columns), f32),
            dma((chunks,)),
            dma((chunks,)),
            dma((chunks,)),
            dma((chunks, pairs - 1)),
            dma((chunks, pairs - 1)),
            dma((2, 2)),
            dma((2, pairs - 1)),
            dma((2, pairs - 1)),
            dma((2,)),
            dma((query_chunks,)),
            dma((query_chunks, 2 * pairs)),
            dma((query_chunks, pairs)),
            dma((query_chunks, pairs)),
            dma((query_chunks, pairs)),
            dma((2,)),
        ],
        compiler_params=pltpu.CompilerParams(
            collective_id=0, has_side_effects=True, vmem_limit_bytes=62 * MIB
        ),
        cost_estimate=pl.CostEstimate(
            flops=4 * total_rows * depth * chunks * width,
            bytes_accessed=2 * depth * chunks * width + 4 * rows * span * width,
            transcendentals=rows * head_count * span,
        ),
    )(
        lengths,
        lengths[None, :],
        request_of_slot[None, :],
        tokens,
        gain[None, :],
        bias_query[None, :],
        bias_key[None, :],
        bias_value[None, :],
        w_query,
        w_key,
        w_value,
        w_output,
        cache_keys,
        cache_values,
    )


def solution(mesh):
    in_specs = (
        P("groups", "pool"),
        P("pool"),
        P("pool", "tp"),
        P("pool", "tp"),
        P("pool", "tp"),
        P("tp"),
        P("tp"),
        P("tp"),
        P("tp", "pool"),
        P(("groups", "pool"), None, "tp"),
        P(("groups", "pool"), None, "tp"),
        P(("groups", "pool")),
        P("groups"),
    )
    out_specs = P(("groups", "tp"), "pool")
    return jax.shard_map(local, mesh=mesh, in_specs=in_specs, out_specs=out_specs, check_vma=False)
```
